32 devices in a mesh: rep: 16 (over z, y, core), fsdp: 2 (over x).
Axes of the slice: x: 2, y: 2, z: 4, core: 2. Of those that a mesh axis runs over, the one named last changes fastest.
Arguments:
- inputs: bfloat16 [16, 768, 2560], P('rep', 'fsdp'), may hold values from -6 to 6
- cotangent: bfloat16 [16, 768, 2560], P('rep', 'fsdp'), may hold values from -0.119628906 to 0.119628906
- params: float32 [16, 2560, 2560], P('rep', 'fsdp'), may hold values from -3 to 3
- momentum: bfloat16 [16, 2560, 2560], P('rep', 'fsdp'), may hold values from -6 to 6
- step: int32 [1], replicated, may hold values from 0 to 999
Outputs:
- new_params: float32 [16, 2560, 2560], P('rep', 'fsdp')
- new_momentum: bfloat16 [16, 2560, 2560], P('rep', 'fsdp')
The draws below stay inside these ranges and needn't reach their ends.
All inputs are finite; a program needn't handle non-finite values.
Results may differ from the reference program's by a relative error of at most 0.014.
Values may be sent and summed in bfloat16 or wider, within the bound.
A program may use at most 192 MiB of HBM per device.

```python
import jax
import jax.numpy as jnp
from jax import lax

D = 2560
QW = 2560
REPS = 16
LEVELS = 4
ROWS = 768


def block_levels(own_key, extent, split, least, largest):
    def one(position, shards_of):
        heights = jax.random.uniform(jax.random.fold_in(jax.random.fold_in(own_key, 6), position), (shards_of,), jnp.float32, least / len(split), largest / len(split))
        return jnp.repeat(jnp.exp(heights), extent[position] // shards_of).reshape((-1,) + (1,) * (len(extent) - position - 1))

    gain = one(*split[0])
    for cut in split[1:]:
        gain = gain * one(*cut)
    return gain


def normal_values(rng, extent, width, reach, shards=(), held_as=jnp.bfloat16):
    array = jax.random.normal(rng, extent, jnp.float32) * width
    if len(shards) > 0:
        array = block_levels(rng, extent, shards, -0.22, 0.18) * array
    return jnp.clip(array, min=-reach, max=reach).astype(held_as)


def setup_inputs(seed: int = 0) -> dict:
    splits = jax.random.split(jax.random.key(seed), 6)
    return {
        "inputs": normal_values(splits[0], (REPS, ROWS, D), 1.0, 6.0, ((0, 16), (1, 2))),
        "cotangent": normal_values(splits[1], (REPS, ROWS, QW), 0.02, 0.119628906, ((0, 16), (1, 2))),
        "params": normal_values(splits[2], (REPS, D, QW), 0.5, 3.0, ((0, 16), (1, 2)), jnp.float32),
        "momentum": normal_values(splits[3], (REPS, D, QW), 1.0, 6.0, ((0, 16), (1, 2))),
        "step": jax.random.randint(splits[4], (1,), 0, 1000).astype(jnp.int32),
    }


learn_rate = 0.1
decay_factor = 0.9

def normalize(activations):
    values = activations.astype(jnp.float32)
    scale = lax.rsqrt(lax.optimization_barrier(jnp.mean(values * values, axis=1, keepdims=True)) + 1e-05)
    return (values * scale).astype(jnp.bfloat16)

def reference(inputs, cotangent, params, momentum, step):
    bit_number = step[0] % LEVELS
    offset = jnp.left_shift(jnp.int32(1), bit_number.astype(jnp.int32))

    def one_replica(replica):
        partner = jnp.bitwise_xor(replica, offset).astype(jnp.int32)
        normed = normalize(inputs[replica])
        grad = lax.dot_general(normed, cotangent[replica], (((0,), (0,)), ((), ())), preferred_element_type=jnp.float32)
        mixed_params = 0.5 * (params[replica] + params[partner])
        mixed_momentum = 0.5 * (momentum[replica].astype(jnp.float32) + momentum[partner].astype(jnp.float32))
        moment = decay_factor * mixed_momentum + grad
        updated = mixed_params - learn_rate * moment
        return (updated, moment.astype(jnp.bfloat16))
    new_params, new_momentum = lax.map(one_replica, jnp.arange(REPS, dtype=jnp.int32))
    return (new_params, new_momentum)
```

```python
import functools

import jax
import jax.numpy as jnp
from jax import lax
from jax.experimental import pallas as pl
from jax.experimental.pallas import tpu as pltpu
from jax.sharding import PartitionSpec as P

learn_rate = 0.1
decay_factor = 0.9
lag = 3


def swap_route(count, level):
    return [(i, i ^ (1 << level)) for i in range(count)]


def shift_route(count, shift):
    return [(i, (i + shift) % count) for i in range(count)]


def normalize(activations):
    values = activations.astype(jnp.float32)
    scale = lax.rsqrt(jnp.mean(values * values, axis=1, keepdims=True) + 1e-05)
    return (values * scale).astype(jnp.bfloat16)


def moment_kernel(shards, *refs):
    normed = refs[:shards]
    grads = refs[shards : 2 * shards]
    params, momentum, other_moment = refs[2 * shards : 2 * shards + 3]
    part_params, new_moment = refs[-2:]
    total = None
    for left, right in zip(normed, grads):
        part = lax.dot_general(
            left[...], right[...], (((0,), (0,)), ((), ())), preferred_element_type=jnp.float32
        )
        total = part if total is None else total + part
    mixed_moment = 0.5 * (
        momentum[...].astype(jnp.float32) + other_moment[...].astype(jnp.float32)
    )
    moment = decay_factor * mixed_moment + total
    part_params[...] = 0.5 * params[...] - learn_rate * moment
    new_moment[...] = moment.astype(jnp.bfloat16)


def widest(cols, choices):
    for candidate in choices:
        if cols % candidate == 0:
            return candidate
    return cols


def moment_chunk(index, normed, grads, params, momentum, other_moment, outs):
    shards = len(normed)
    rows, cols = other_moment.shape
    tokens = grads[0].shape[0]
    wide = widest(cols, (640, 512))
    own = pl.BlockSpec((rows, wide), lambda j: (index, j))
    other = pl.BlockSpec((rows, wide), lambda j: (0, j))
    in_specs = (
        [pl.BlockSpec((tokens, rows), lambda j: (0, 0))] * shards
        + [pl.BlockSpec((tokens, wide), lambda j: (0, j))] * shards
        + [own, own, other]
    )
    args = [*normed, *grads, params, momentum, other_moment]
    aliases = {}
    if outs is not None:
        in_specs += [pl.BlockSpec(memory_space=pl.ANY)] * 2
        aliases = {len(args): 0, len(args) + 1: 1}
        args += list(outs)
    return pl.pallas_call(
        functools.partial(moment_kernel, shards),
        grid=(cols // wide,),
        out_shape=[
            jax.ShapeDtypeStruct(params.shape, params.dtype),
            jax.ShapeDtypeStruct(momentum.shape, momentum.dtype),
        ],
        in_specs=in_specs,
        out_specs=[own, own],
        input_output_aliases=aliases,
        cost_estimate=pl.CostEstimate(
            flops=2 * shards * tokens * rows * cols,
            bytes_accessed=rows * cols * 14 + shards * tokens * (rows + cols) * 2,
            transcendentals=0,
        ),
        compiler_params=pltpu.CompilerParams(vmem_limit_bytes=56 << 20),
    )(*args)


def mix_kernel(part_params, other_params, new_params):
    new_params[...] = part_params[...] + 0.5 * other_params[...].astype(jnp.float32)


def mix_chunk(index, part_params, other_params):
    rows, cols = other_params.shape
    high = widest(rows, (64,))
    steps = rows // high
    own = pl.BlockSpec((high, cols), lambda i: (index * steps + i, 0))
    return pl.pallas_call(
        mix_kernel,
        grid=(steps,),
        out_shape=jax.ShapeDtypeStruct(part_params.shape, part_params.dtype),
        in_specs=[own, pl.BlockSpec((high, cols), lambda i: (i, 0))],
        out_specs=own,
        input_output_aliases={0: 0},
        cost_estimate=pl.CostEstimate(
            flops=2 * rows * cols, bytes_accessed=rows * cols * 10, transcendentals=0
        ),
        compiler_params=pltpu.CompilerParams(vmem_limit_bytes=56 << 20),
    )(part_params, other_params)


def chunk_height(rows):
    return widest(rows, (256,))


def after(value, *others):
    return lax.optimization_barrier((value, *others))[0]


def make_branch(level):

    def branch(inputs, cotangent, params, momentum):
        shards = lax.axis_size("fsdp")
        place = lax.axis_index("fsdp")
        rows = params.shape[0]
        height = chunk_height(rows)
        count = rows // height
        swap = swap_route(lax.axis_size("rep"), level)
        arrived = []
        for k in range(count):
            piece = momentum[k * height : (k + 1) * height]
            if k >= lag:
                piece = after(piece, arrived[k - lag])
            arrived.append(lax.ppermute(piece, "rep", swap))
        for k in range(count):
            piece = params[k * height : (k + 1) * height]
            if count + k >= lag:
                piece = after(piece, arrived[count + k - lag])
            arrived.append(lax.ppermute(piece.astype(jnp.bfloat16), "rep", swap))
        other_moment, other_params = arrived[:count], arrived[count:]
        grads = [cotangent]
        for shift in range(1, shards):
            grads.append(lax.ppermute(cotangent, "fsdp", shift_route(shards, shift)))
        normed = normalize(inputs)
        outs = None
        for k in range(count):
            pieces = [lax.dynamic_slice_in_dim(normed, place * rows + k * height, height, 1)]
            for shift in range(1, shards):
                target = lax.rem(place + shift, shards)
                piece = lax.dynamic_slice_in_dim(normed, target * rows + k * height, height, 1)
                pieces.append(lax.ppermute(piece, "fsdp", shift_route(shards, shift)))
            outs = moment_chunk(k, pieces, grads, params, momentum, other_moment[k], outs)
        part_params, new_momentum = outs
        for k in range(count - 1):
            part_params = mix_chunk(k, part_params, other_params[k])
        return part_params, new_momentum, other_params[-1]

    return branch


def on_device(inputs, cotangent, params, momentum, step):
    level_count = lax.axis_size("rep").bit_length() - 1
    branches = [make_branch(level) for level in range(level_count)]
    part_params, new_momentum, last = lax.switch(
        step[0] % level_count, branches, inputs[0], cotangent[0], params[0], momentum[0]
    )
    new_params = mix_chunk(part_params.shape[0] // last.shape[0] - 1, part_params, last)
    return (new_params[None], new_momentum[None])


def solution(mesh):
    in_specs = (
        P("rep", "fsdp", None),
        P("rep", "fsdp", None),
        P("rep", "fsdp", None),
        P("rep", "fsdp", None),
        P(),
    )
    out_specs = (P("rep", "fsdp", None), P("rep", "fsdp", None))
    return jax.shard_map(
        on_device, mesh=mesh, in_specs=in_specs, out_specs=out_specs, check_vma=False
    )
```

```python
import functools

import jax
import jax.numpy as jnp
from jax import lax
from jax.experimental import pallas as pl
from jax.experimental.pallas import tpu as pltpu
from jax.sharding import PartitionSpec as P

learn_rate = 0.1
decay_factor = 0.9
lag = 3


def swap_route(count, level):
    return [(i, i ^ (1 << level)) for i in range(count)]


def shift_route(count, shift):
    return [(i, (i + shift) % count) for i in range(count)]


def normalize(activations):
    values = activations.astype(jnp.float32)
    scale = lax.rsqrt(jnp.mean(values * values, axis=1, keepdims=True) + 1e-05)
    return (values * scale).astype(jnp.bfloat16)


def moment_kernel(shards, whole, *refs):
    normed = refs[:shards]
    grads = refs[shards : 2 * shards]
    params, momentum, other_moment = refs[2 * shards : 2 * shards + 3]
    part_params, new_moment = refs[-2:]
    total = None
    for left, right in zip(normed, grads):
        part = lax.dot_general(
            left[...], right[...], (((0,), (0,)), ((), ())), preferred_element_type=jnp.float32
        )
        total = part if total is None else total + part
    mixed_moment = 0.5 * (
        momentum[...].astype(jnp.float32) + other_moment[...].astype(jnp.float32)
    )
    moment = decay_factor * mixed_moment + total
    mixed_params = params[...]
    if whole:
        mixed_params = mixed_params + refs[2 * shards + 3][...].astype(jnp.float32)
    part_params[...] = 0.5 * mixed_params - learn_rate * moment
    new_moment[...] = moment.astype(jnp.bfloat16)


def widest(cols, choices):
    for candidate in choices:
        if cols % candidate == 0:
            return candidate
    return cols


def moment_chunk(index, normed, grads, params, momentum, other_moment, outs, other_params=None):
    shards = len(normed)
    whole = other_params is not None
    tokens, rows = normed[0].shape
    cols = params.shape[1]
    wide = widest(cols, (256,) if whole else (640, 512))
    own = pl.BlockSpec((rows, wide), lambda j: (index, j))
    other = own if whole else pl.BlockSpec((rows, wide), lambda j: (0, j))
    in_specs = (
        [pl.BlockSpec((tokens, rows), lambda j: (0, 0))] * shards
        + [pl.BlockSpec((tokens, wide), lambda j: (0, j))] * shards
        + [own, own, other]
    )
    args = [*normed, *grads, params, momentum, other_moment]
    if whole:
        in_specs.append(own)
        args.append(other_params)
    aliases = {}
    if outs is not None:
        in_specs += [pl.BlockSpec(memory_space=pl.ANY)] * 2
        aliases = {len(args): 0, len(args) + 1: 1}
        args += list(outs)
    return pl.pallas_call(
        functools.partial(moment_kernel, shards, whole),
        grid=(cols // wide,),
        out_shape=[
            jax.ShapeDtypeStruct(params.shape, params.dtype),
            jax.ShapeDtypeStruct(momentum.shape, momentum.dtype),
        ],
        in_specs=in_specs,
        out_specs=[own, own],
        input_output_aliases=aliases,
        cost_estimate=pl.CostEstimate(
            flops=2 * shards * tokens * rows * cols,
            bytes_accessed=rows * cols * 14 + shards * tokens * (rows + cols) * 2,
            transcendentals=0,
        ),
        compiler_params=pltpu.CompilerParams(vmem_limit_bytes=56 << 20),
    )(*args)


def mix_kernel(part_params, other_params, new_params):
    new_params[...] = part_params[...] + 0.5 * other_params[...].astype(jnp.float32)


def mix_chunk(begin, part_params, other_params):
    rows, cols = other_params.shape
    high = widest(rows, (32,) if rows <= 64 else (64,))
    steps = rows // high
    own = pl.BlockSpec((high, cols), lambda i: (begin // high + i, 0))
    return pl.pallas_call(
        mix_kernel,
        grid=(steps,),
        out_shape=jax.ShapeDtypeStruct(part_params.shape, part_params.dtype),
        in_specs=[own, pl.BlockSpec((high, cols), lambda i: (i, 0))],
        out_specs=own,
        input_output_aliases={0: 0},
        cost_estimate=pl.CostEstimate(
            flops=2 * rows * cols, bytes_accessed=rows * cols * 10, transcendentals=0
        ),
        compiler_params=pltpu.CompilerParams(vmem_limit_bytes=56 << 20),
    )(part_params, other_params)


def chunk_heights(rows):
    height = widest(rows, (256,))
    heights = [height] * (rows // height)
    if height > 64 and height % 64 == 0:
        heights[-1:] = [height - 64, 64]
    return heights


def after(value, *others):
    return lax.optimization_barrier((value, *others))[0]


def swap_columns(normed, start, width, rows):
    shards = lax.axis_size("fsdp")
    place = lax.axis_index("fsdp")
    pieces = [lax.dynamic_slice_in_dim(normed, place * rows + start, width, 1)]
    for shift in range(1, shards):
        target = lax.rem(place + shift, shards)
        piece = lax.dynamic_slice_in_dim(normed, target * rows + start, width, 1)
        pieces.append(lax.ppermute(piece, "fsdp", shift_route(shards, shift)))
    return pieces


def swap_gradients(cotangent):
    shards = lax.axis_size("fsdp")
    return [cotangent] + [
        lax.ppermute(cotangent, "fsdp", shift_route(shards, shift)) for shift in range(1, shards)
    ]


def make_near_branch(level):

    def branch(inputs, cotangent, params, momentum):
        rows, cols = params.shape
        height = widest(rows, (640,))
        swap = swap_route(lax.axis_size("rep"), level)
        grads = swap_gradients(cotangent)
        normed = normalize(inputs)
        pieces = [swap_columns(normed, k * height, height, rows) for k in range(rows // height)]
        other_moment = lax.ppermute(momentum, "rep", swap)
        other_params = lax.ppermute(
            after(params, other_moment).astype(jnp.bfloat16), "rep", swap
        )
        outs = None
        for k, piece in enumerate(pieces):
            outs = moment_chunk(
                k, piece, grads, params, momentum, other_moment, outs, other_params
            )
        return *outs, jnp.zeros((chunk_heights(rows)[-1], cols), jnp.bfloat16)

    return branch


def make_far_branch(level):

    def branch(inputs, cotangent, params, momentum):
        rows = params.shape[0]
        height = widest(rows, (256,))
        count = rows // height
        swap = swap_route(lax.axis_size("rep"), level)
        arrived = []
        source = momentum
        for k in range(count):
            piece = source[k * height : (k + 1) * height]
            if k == 0:
                source = after(momentum, piece)
            if k >= lag:
                piece = after(piece, arrived[k - lag])
            arrived.append(lax.ppermute(piece, "rep", swap))
        grads = swap_gradients(cotangent)
        normed = normalize(inputs)
        pieces = [swap_columns(normed, k * height, height, rows) for k in range(count)]
        begin = 0
        heights = chunk_heights(rows)
        for k, high in enumerate(heights):
            piece = params[begin : begin + high]
            begin += high
            waits = [arrived[max(count + k - lag, 0)], grads[-1]]
            if k > 0:
                waits += [part[-1] for part in pieces]
            arrived.append(
                lax.ppermute(after(piece, *waits).astype(jnp.bfloat16), "rep", swap)
            )
        outs = None
        for k in range(count):
            outs = moment_chunk(k, pieces[k], grads, params, momentum, arrived[k], outs)
        part_params, new_momentum = outs
        begin = 0
        for high, other_params in zip(heights[:-1], arrived[count:-1]):
            part_params = mix_chunk(begin, part_params, other_params)
            begin += high
        return part_params, new_momentum, arrived[-1]

    return branch


def on_device(inputs, cotangent, params, momentum, step):
    level_count = lax.axis_size("rep").bit_length() - 1
    branches = [make_far_branch(level) if level else make_near_branch(level) for level in range(level_count)]
    part_params, new_momentum, last = lax.switch(
        step[0] % level_count, branches, inputs[0], cotangent[0], params[0], momentum[0]
    )
    new_params = mix_chunk(part_params.shape[0] - last.shape[0], part_params, last)
    return (new_params[None], new_momentum[None])


def solution(mesh):
    in_specs = (
        P("rep", "fsdp", None),
        P("rep", "fsdp", None),
        P("rep", "fsdp", None),
        P("rep", "fsdp", None),
        P(),
    )
    out_specs = (P("rep", "fsdp", None), P("rep", "fsdp", None))
    return jax.shard_map(
        on_device, mesh=mesh, in_specs=in_specs, out_specs=out_specs, check_vma=False
    )
```

```python
import functools

import jax
import jax.numpy as jnp
from jax import lax
from jax.experimental import pallas as pl
from jax.experimental.pallas import tpu as pltpu
from jax.sharding import PartitionSpec as P

learn_rate = 0.1
decay_factor = 0.9
lag = 3


def swap_route(count, level):
    return [(i, i ^ (1 << level)) for i in range(count)]


def shift_route(count, shift):
    return [(i, (i + shift) % count) for i in range(count)]


def normalize(activations):
    values = activations.astype(jnp.float32)
    scale = lax.rsqrt(jnp.mean(values * values, axis=1, keepdims=True) + 1e-05)
    return (values * scale).astype(jnp.bfloat16)


def moment_kernel(shards, whole, *refs):
    normed = refs[:shards]
    grads = refs[shards : 2 * shards]
    params, momentum, other_moment = refs[2 * shards : 2 * shards + 3]
    part_params, new_moment = refs[-2:]
    total = None
    for left, right in zip(normed, grads):
        part = lax.dot_general(
            left[...], right[...], (((0,), (0,)), ((), ())), preferred_element_type=jnp.float32
        )
        total = part if total is None else total + part
    mixed_moment = 0.5 * (
        momentum[...].astype(jnp.float32) + other_moment[...].astype(jnp.float32)
    )
    moment = decay_factor * mixed_moment + total
    mixed_params = params[...]
    if whole:
        mixed_params = mixed_params + refs[2 * shards + 3][...].astype(jnp.float32)
    part_params[...] = 0.5 * mixed_params - learn_rate * moment
    new_moment[...] = moment.astype(jnp.bfloat16)


def widest(cols, choices):
    for candidate in choices:
        if cols % candidate == 0:
            return candidate
    return cols


def moment_chunk(index, normed, grads, params, momentum, other_moment, outs, other_params=None):
    shards = len(normed)
    whole = other_params is not None
    tokens, rows = normed[0].shape
    cols = params.shape[1]
    wide = widest(cols, (256,) if whole else (640, 512))
    own = pl.BlockSpec((rows, wide), lambda j: (index, j))
    other = own if whole else pl.BlockSpec((rows, wide), lambda j: (0, j))
    in_specs = (
        [pl.BlockSpec((tokens, rows), lambda j: (0, 0))] * shards
        + [pl.BlockSpec((tokens, wide), lambda j: (0, j))] * shards
        + [own, own, other]
    )
    args = [*normed, *grads, params, momentum, other_moment]
    if whole:
        in_specs.append(own)
        args.append(other_params)
    aliases = {}
    if outs is not None:
        in_specs += [pl.BlockSpec(memory_space=pl.ANY)] * 2
        aliases = {len(args): 0, len(args) + 1: 1}
        args += list(outs)
    return pl.pallas_call(
        functools.partial(moment_kernel, shards, whole),
        grid=(cols // wide,),
        out_shape=[
            jax.ShapeDtypeStruct(params.shape, params.dtype),
            jax.ShapeDtypeStruct(momentum.shape, momentum.dtype),
        ],
        in_specs=in_specs,
        out_specs=[own, own],
        input_output_aliases=aliases,
        cost_estimate=pl.CostEstimate(
            flops=2 * shards * tokens * rows * cols,
            bytes_accessed=rows * cols * 14 + shards * tokens * (rows + cols) * 2,
            transcendentals=0,
        ),
        compiler_params=pltpu.CompilerParams(vmem_limit_bytes=56 << 20),
    )(*args)


def mix_kernel(part_params, other_params, new_params):
    new_params[...] = part_params[...] + 0.5 * other_params[...].astype(jnp.float32)


def mix_chunk(begin, part_params, other_params):
    rows, cols = other_params.shape
    high = widest(rows, (32,) if rows <= 64 else (64,))
    steps = rows // high
    own = pl.BlockSpec((high, cols), lambda i: (begin // high + i, 0))
    return pl.pallas_call(
        mix_kernel,
        grid=(steps,),
        out_shape=jax.ShapeDtypeStruct(part_params.shape, part_params.dtype),
        in_specs=[own, pl.BlockSpec((high, cols), lambda i: (i, 0))],
        out_specs=own,
        input_output_aliases={0: 0},
        cost_estimate=pl.CostEstimate(
            flops=2 * rows * cols, bytes_accessed=rows * cols * 10, transcendentals=0
        ),
        compiler_params=pltpu.CompilerParams(vmem_limit_bytes=56 << 20),
    )(part_params, other_params)


def chunk_heights(rows):
    height = widest(rows, (256,))
    heights = [height] * (rows // height)
    if height > 64 and height % 64 == 0:
        heights[-1:] = [height - 64, 64]
    return heights


def after(value, *others):
    return lax.optimization_barrier((value, *others))[0]


def swap_columns(normed, start, width, rows):
    shards = lax.axis_size("fsdp")
    place = lax.axis_index("fsdp")
    pieces = [lax.dynamic_slice_in_dim(normed, place * rows + start, width, 1)]
    for shift in range(1, shards):
        target = lax.rem(place + shift, shards)
        piece = lax.dynamic_slice_in_dim(normed, target * rows + start, width, 1)
        pieces.append(lax.ppermute(piece, "fsdp", shift_route(shards, shift)))
    return pieces


def swap_gradients(cotangent):
    shards = lax.axis_size("fsdp")
    return [cotangent] + [
        lax.ppermute(cotangent, "fsdp", shift_route(shards, shift)) for shift in range(1, shards)
    ]


def make_near_branch(level):

    def branch(inputs, cotangent, params, momentum):
        rows, cols = params.shape
        height = widest(rows, (640,))
        swap = swap_route(lax.axis_size("rep"), level)
        grads = swap_gradients(cotangent)
        normed = normalize(inputs)
        pieces = [swap_columns(normed, k * height, height, rows) for k in range(rows // height)]
        other_moment = lax.ppermute(momentum, "rep", swap)
        other_params = lax.ppermute(
            after(params, grads[-1]).astype(jnp.bfloat16), "rep", swap
        )
        outs = None
        for k, piece in enumerate(pieces):
            outs = moment_chunk(
                k, piece, grads, params, momentum, other_moment, outs, other_params
            )
        return *outs, jnp.zeros((chunk_heights(rows)[-1], cols), jnp.bfloat16)

    return branch


def make_far_branch(level):

    def branch(inputs, cotangent, params, momentum):
        rows = params.shape[0]
        height = widest(rows, (256,))
        count = rows // height
        swap = swap_route(lax.axis_size("rep"), level)
        arrived = []
        source = momentum
        for k in range(count):
            piece = source[k * height : (k + 1) * height]
            if k == 0:
                source = after(momentum, piece)
            if k >= lag:
                piece = after(piece, arrived[k - lag])
            arrived.append(lax.ppermute(piece, "rep", swap))
        grads = swap_gradients(cotangent)
        normed = normalize(inputs)
        pieces = [swap_columns(normed, k * height, height, rows) for k in range(count)]
        begin = 0
        heights = chunk_heights(rows)
        for k, high in enumerate(heights):
            piece = params[begin : begin + high]
            begin += high
            waits = [arrived[max(count + k - lag, 0)], grads[-1]]
            if k > 0:
                waits += [part[-1] for part in pieces]
            arrived.append(
                lax.ppermute(after(piece, *waits).astype(jnp.bfloat16), "rep", swap)
            )
        outs = None
        for k in range(count):
            outs = moment_chunk(k, pieces[k], grads, params, momentum, arrived[k], outs)
        part_params, new_momentum = outs
        begin = 0
        for high, other_params in zip(heights[:-1], arrived[count:-1]):
            part_params = mix_chunk(begin, part_params, other_params)
            begin += high
        return part_params, new_momentum, arrived[-1]

    return branch


def on_device(inputs, cotangent, params, momentum, step):
    level_count = lax.axis_size("rep").bit_length() - 1
    branches = [make_far_branch(level) if level else make_near_branch(level) for level in range(level_count)]
    part_params, new_momentum, last = lax.switch(
        step[0] % level_count, branches, inputs[0], cotangent[0], params[0], momentum[0]
    )
    new_params = mix_chunk(part_params.shape[0] - last.shape[0], part_params, last)
    return (new_params[None], new_momentum[None])


def solution(mesh):
    in_specs = (
        P("rep", "fsdp", None),
        P("rep", "fsdp", None),
        P("rep", "fsdp", None),
        P("rep", "fsdp", None),
        P(),
    )
    out_specs = (P("rep", "fsdp", None), P("rep", "fsdp", None))
    return jax.shard_map(
        on_device, mesh=mesh, in_specs=in_specs, out_specs=out_specs, check_vma=False
    )
```
